32 devices in a mesh: section: 4 (over z), expert: 2 (over y), mp: 4 (over x, core).
Axes of the slice: x: 2, y: 2, z: 4, core: 2. Of those that a mesh axis runs over, the one named last changes fastest.
Arguments:
- grad_in: bfloat16 [4, 256, 3072], P('section', 'expert', 'mp'), may hold values from -6 to 6
- saved_input: bfloat16 [4, 2, 256, 3072], P('section', None, 'expert', 'mp'), may hold values from -6 to 6
- routes: int32 [4, 2, 256, 2], P('section', None, 'expert'), may hold values from 0 to 3, all different within a row; in each aligned block of 128 rows (0 to 127, 128 to 255, ..., all dimensions but the last counted through in order) at most 72 rows name the same one
- route_weights: float32 [4, 2, 256, 2], P('section', None, 'expert'), may hold values from 0.2 to 1
- plan: int32 [4, 2], P('section'), may hold values from 0 to 1, each once within a row
- up_weight: bfloat16 [4, 3072, 32768], P('section', None, ('expert', 'mp')), may hold values from -0.109375 to 0.109375
- down_weight: bfloat16 [4, 32768, 3072], P('section', ('expert', 'mp')), may hold values from -0.0625 to 0.0625
Outputs:
- passed_grad: bfloat16 [4, 256, 3072], P('section', 'expert', 'mp')
The draws below stay inside these ranges and needn't reach their ends.
Inputs may be any that keep to these rules, and one draw needn't show every extreme that they name: `routes`: the numbers of a row differ. In each aligned block of 128 rows (the rows of one index of expert within one section and microbatch) no expert is named by more than 72 rows, and some block reaches 72. `plan`: each row is a permutation of 0 to 1.
All inputs are finite; a program needn't handle non-finite values.
Results may differ from the reference program's by a relative error of at most 0.0065.
Values may be sent and summed in bfloat16 or wider, within the bound.
A program may use at most 128 MiB of HBM per device.

```python
import math
import jax
import jax.numpy as jnp
import numpy as np
from jax import lax

D = 3072
FF = 8192
EXPERTS = 4
TOP = 2
MICRO = 2
ROWS_DEV = 128
CAPACITY = 72
SECTIONS = 4
GROUP_ROWS = 256
N_EXPERT = 2


def block_levels(rng, extent, pieces, least, high):
    factor_of = 1.0
    for dim, shards_of in pieces:
        draws = jax.random.uniform(jax.random.fold_in(jax.random.fold_in(rng, 6), dim), (shards_of,), jnp.float32, least / len(pieces), high / len(pieces))
        factor_of = factor_of * jnp.repeat(jnp.exp(draws), extent[dim] // shards_of).reshape((-1,) + (1,) * (len(extent) - 1 - dim))
    return factor_of


def routed_block(stream_key, own, number, rows, count, top, reach, skew):
    ranking = jax.random.permutation(stream_key, count)
    heavy_load, common = shares(count, rows * top, reach, skew, True), shares(count, rows * top, reach, skew, False)
    places = jnp.arange(count)

    def named(tallies, rotation):
        used = int((tallies > 0).sum())
        fixed = max(1, used // 4)
        passed = fixed + (places - fixed + rotation * (used - fixed)) % max(1, count - fixed)
        return jnp.zeros((count,), jnp.int32).at[ranking[jnp.where(places < fixed, places, passed)]].set(jnp.asarray(tallies, jnp.int32))

    tallies = jnp.where(number % 4 == 0, named(heavy_load, number // 4), named(common, number - number // 4 - 1))
    mixed = jax.random.permutation(jax.random.fold_in(own, 3), count)
    giver, receiver = mixed[0:count // 2 * 2:2], mixed[1:count // 2 * 2:2]
    slack = jnp.minimum(tallies[giver] - 1, reach - tallies[receiver]) // 2
    slack = jnp.where((giver == ranking[0]) | (receiver == ranking[0]) | (tallies[receiver] == 0), 0, jnp.maximum(slack, 0))
    passed = jax.random.randint(jax.random.fold_in(own, 4), (count // 2,), 0, 1 << 20) % (slack + 1)
    tallies = tallies.at[giver].add(-passed).at[receiver].add(passed)
    items = jnp.searchsorted(jnp.cumsum(tallies), jnp.arange(rows * top), side="right").astype(jnp.int32)
    grid = items.reshape(top, rows).T
    grid = grid[jax.random.permutation(jax.random.fold_in(own, 1), rows)]
    rotation = jax.random.randint(jax.random.fold_in(own, 2), (rows, 1), 0, top)
    return jnp.take_along_axis(grid, (jnp.arange(top)[None, :] + rotation) % top, axis=1)


def shares(amount, total, most, skew, full):
    portions = [(1 << 20) // math.isqrt(rank ** skew) + 1 for rank in range(1, amount + 1)]
    largest = most if full else min(most, max(-(-total // amount), total * portions[0] // sum(portions)))
    least = 1 if total - largest >= amount - 1 else 0
    given, rest = [largest] + [least] * (amount - 1), total - largest - least * (amount - 1)
    while rest > 0:
        candidates = [i for i in range(1, amount) if given[i] < largest] or [i for i in range(1, amount) if given[i] < most]
        whole, left = sum([portions[i] for i in candidates]), rest
        for i in candidates:
            more = min(most - given[i], max(1, left * portions[i] // whole), rest)
            given[i] = given[i] + more
            rest = rest - more
    return np.array(given)


def centred(stream_key, dims, width, reach, cuts=(), kind=jnp.bfloat16):
    values = jax.random.normal(stream_key, dims, jnp.float32) * width
    if len(cuts) > 0:
        values = block_levels(stream_key, dims, cuts, -0.22, 0.18) * values
    return jnp.clip(values, min=-reach, max=reach).astype(kind)


def setup_inputs(seed: int = 0) -> dict:
    arg_keys = jax.random.split(jax.random.key(seed), 8)
    grad_in = centred(arg_keys[0], (SECTIONS, GROUP_ROWS, D), 1.0, 6.0, ((0, 4), (1, 2), (2, 4)))
    saved_input = centred(arg_keys[1], (SECTIONS, MICRO, GROUP_ROWS, D), 1.0, 6.0, ((0, 4), (2, 2), (3, 4)))
    routes_keys = jax.random.split(jax.random.fold_in(arg_keys[2], 1), SECTIONS * MICRO * GROUP_ROWS // ROWS_DEV)
    routes_turns = jax.random.permutation(jax.random.fold_in(arg_keys[2], 3), SECTIONS * MICRO * GROUP_ROWS // ROWS_DEV)
    routes = jax.vmap(lambda own, number: routed_block(jax.random.fold_in(arg_keys[2], 2), own, number, ROWS_DEV, EXPERTS, TOP, CAPACITY, 2))(routes_keys, routes_turns).reshape((SECTIONS, MICRO, GROUP_ROWS, TOP))
    route_weights = jnp.clip(0.2 + 0.8 * jax.random.uniform(arg_keys[3], (SECTIONS, MICRO, GROUP_ROWS, TOP), jnp.float32) ** block_levels(arg_keys[3], (SECTIONS, MICRO, GROUP_ROWS, TOP), ((0, 4), (2, 2)), -0.2, 0.2), 0.2, 1.0)
    plan = jax.vmap(lambda own: jax.random.permutation(own, MICRO))(jax.random.split(arg_keys[4], SECTIONS)).reshape((SECTIONS, MICRO)).astype(jnp.int32)
    up_weight = centred(arg_keys[5], (SECTIONS, D, EXPERTS * FF), D ** -0.5, 0.109375, ((0, 4), (2, 8)))
    down_weight = centred(arg_keys[6], (SECTIONS, EXPERTS * FF, D), FF ** -0.5, 0.0625, ((0, 4), (1, 8)))
    return {"grad_in": grad_in, "saved_input": saved_input, "routes": routes, "route_weights": route_weights, "plan": plan, "up_weight": up_weight, "down_weight": down_weight}


def slot_targets(route_now):
    blocks = route_now.reshape(N_EXPERT, ROWS_DEV, TOP)
    expert_ids = jnp.arange(EXPERTS, dtype=jnp.int32)
    onehot = (blocks[..., None] == expert_ids).astype(jnp.int32)
    counts = jnp.sum(onehot, axis=2)
    before = jnp.cumsum(counts, axis=1) - counts
    slot_pos = jnp.sum(before[:, :, None, :] * onehot, axis=3)
    return (blocks * CAPACITY + slot_pos).astype(jnp.int32)


def expert_back(operands):
    expert_id, rows_in, grads_in, up_all, down_all = operands
    start = (expert_id * FF).astype(jnp.int32)
    up_cols = lax.dynamic_slice_in_dim(up_all, start, FF, 1)
    down_rows = lax.dynamic_slice_in_dim(down_all, start, FF, 0)
    pre_act = jnp.dot(rows_in, up_cols, preferred_element_type=jnp.float32)
    grad_act = jnp.dot(grads_in, down_rows.T, preferred_element_type=jnp.float32)
    sigma_up = jax.nn.sigmoid(pre_act)
    grad_pre = (grad_act * sigma_up * (1.0 + pre_act * (1.0 - sigma_up))).astype(jnp.bfloat16)
    return jnp.dot(grad_pre, up_cols.T, preferred_element_type=jnp.float32)


def layer_back(grad_rows, saved_rows, route_now, weight_now, up_all, down_all):
    target = slot_targets(route_now)
    group_ids = jnp.broadcast_to(jnp.arange(N_EXPERT, dtype=jnp.int32)[:, None, None], target.shape)
    saved_blocks = saved_rows.reshape(N_EXPERT, ROWS_DEV, D)
    grad_blocks = grad_rows.reshape(N_EXPERT, ROWS_DEV, D)
    saved_rep = jnp.broadcast_to(saved_blocks[:, :, None, :], (N_EXPERT, ROWS_DEV, TOP, D))
    grad_rep = jnp.broadcast_to(grad_blocks[:, :, None, :], (N_EXPERT, ROWS_DEV, TOP, D))
    buffer_in = jnp.zeros((N_EXPERT, EXPERTS * CAPACITY, D), jnp.bfloat16).at[group_ids, target].set(saved_rep)
    buffer_grad = jnp.zeros((N_EXPERT, EXPERTS * CAPACITY, D), jnp.bfloat16).at[group_ids, target].set(grad_rep)

    def by_expert(buffer):
        return buffer.reshape(N_EXPERT, EXPERTS, CAPACITY, D).transpose(1, 0, 2, 3).reshape(EXPERTS, N_EXPERT * CAPACITY, D)

    def one_expert(operands):
        expert_id, rows_in, grads_in = operands
        return expert_back((expert_id, rows_in, grads_in, up_all, down_all))

    branch = lax.map(one_expert, (jnp.arange(EXPERTS, dtype=jnp.int32), by_expert(buffer_in), by_expert(buffer_grad)))
    branch = branch.reshape(EXPERTS, N_EXPERT, CAPACITY, D).transpose(1, 0, 2, 3).reshape(N_EXPERT, EXPERTS * CAPACITY, D)
    picked = branch[group_ids, target]
    weights_blk = weight_now.reshape(N_EXPERT, ROWS_DEV, TOP)
    mixed = jnp.sum(weights_blk[..., None] * picked, axis=2)
    return (grad_blocks.astype(jnp.float32) + mixed).astype(jnp.bfloat16).reshape(GROUP_ROWS, D)


def run_tick(grads, micro_ids, saved_input, routes, route_weights, up_weight, down_weight):
    def section_back(operands):
        grad_rows, saved_s, routes_s, weights_s, micro_index, up_all, down_all = operands

        def select_micro(array):
            return lax.dynamic_index_in_dim(array, micro_index, 0, keepdims=False)

        return layer_back(grad_rows, select_micro(saved_s), select_micro(routes_s), select_micro(weights_s), up_all, down_all)

    return lax.map(section_back, (grads, saved_input, routes, route_weights, micro_ids, up_weight, down_weight))


def reference(grad_in, saved_input, routes, route_weights, plan, up_weight, down_weight):
    first = run_tick(grad_in, plan[:, 0], saved_input, routes, route_weights, up_weight, down_weight)
    second = run_tick(jnp.roll(first, -1, axis=0), plan[:, 1], saved_input, routes, route_weights, up_weight, down_weight)
    return jnp.roll(second, -1, axis=0)
```

```python
import jax
import jax.numpy as jnp
from jax import lax
from jax.experimental import pallas as pl
from jax.experimental.pallas import tpu as pltpu
from jax.sharding import PartitionSpec as P

EXPERTS = 4
CAPACITY = 72
SLOTS = 80
HIDDEN_STEP = 512
FEATURE_STEP = 256
LAST_WITH_LAST = (((1,), (1,)), ((), ()))


def fused_kernel(n_section, grad_ref, saved_ref, routes_ref, shares_ref, plan_ref, up_hbm, down_hbm, out_ref,
                 up, down, saved_rows, grad_rows, factor, pre_grad, sent, part_out, part_in, branch_out, arrived,
                 result, passed, weight_sem, hop_send, hop_recv, twin_send, twin_recv, part_send, part_recv,
                 back_send, back_recv, pass_send, pass_recv):
    section, y, mp = lax.axis_index("section"), lax.axis_index("expert"), lax.axis_index("mp")
    x, core = mp // 2, mp % 2
    quarter = grad_ref.shape[1]
    hidden = up.shape[1]
    steps = hidden // HIDDEN_STEP
    twin = (section, y, x * 2 + 1 - core)
    before = (lax.rem(section + n_section - 1, n_section), y, mp)
    behind = (lax.rem(section + 1, n_section), y, mp)

    def chip(k):
        return lax.rem(y + k // 2, 2), lax.rem(x + k % 2, 2)

    def peer(k):
        py, px = chip(k)
        return (section, py, px * 2 + core)

    def place(py, px, pcore):
        return (pl.ds(pl.multiple_of(py * SLOTS, SLOTS), SLOTS),
                pl.ds(pl.multiple_of((px * 2 + pcore) * quarter, quarter), quarter))

    def slot_rows(py, px):
        return pl.ds(pl.multiple_of((py * 2 + px) * SLOTS, SLOTS), SLOTS)

    def up_copy(i):
        cols = pl.ds(pl.multiple_of(i * HIDDEN_STEP, HIDDEN_STEP), HIDDEN_STEP)
        return pltpu.make_async_copy(up_hbm.at[0, :, cols], up.at[:, cols], weight_sem.at[0, i])

    def down_copy(i):
        rows = pl.ds(pl.multiple_of(i * HIDDEN_STEP, HIDDEN_STEP), HIDDEN_STEP)
        return pltpu.make_async_copy(down_hbm.at[0, rows, :], down.at[rows, :], weight_sem.at[1, i])

    def start_weights(i, carry):
        up_copy(i).start()
        return carry

    def start_weights_down(i, carry):
        down_copy(i).start()
        return carry

    lax.fori_loop(0, steps, start_weights, 0)
    lax.fori_loop(0, steps, start_weights_down, 0)

    barrier = pltpu.get_barrier_semaphore()
    partners = [twin, peer(1), peer(2), peer(3), before, behind]
    for partner in partners:
        pl.semaphore_signal(barrier, inc=1, device_id=partner, device_id_type=pl.DeviceIdType.MESH)

    tokens = routes_ref.shape[1]
    lanes = lax.broadcasted_iota(jnp.int32, (tokens, 128), 1)
    earlier = (lax.broadcasted_iota(jnp.int32, (tokens, tokens), 1)
               < lax.broadcasted_iota(jnp.int32, (tokens, tokens), 0)).astype(jnp.float32).astype(jnp.bfloat16)
    slot_ids = lax.broadcasted_iota(jnp.int32, (tokens, EXPERTS * SLOTS), 1).astype(jnp.float32)

    def micro_is_second(tick):
        return plan_ref[0:1, tick:tick + 1] == 1

    def routing(tick):
        second = jnp.broadcast_to(micro_is_second(tick), (tokens, 2))
        route = jnp.where(second, routes_ref[1], routes_ref[0])
        share = jnp.where(second, shares_ref[1], shares_ref[0])
        hits = [(lanes == route[:, k:k + 1]).astype(jnp.float32) for k in range(2)]
        counts = hits[0] + hits[1]
        ahead = jnp.dot(earlier, counts.astype(jnp.bfloat16), preferred_element_type=jnp.float32)
        mix = jnp.zeros((tokens, EXPERTS * SLOTS), jnp.float32)
        select = jnp.zeros((tokens, EXPERTS * SLOTS), jnp.float32)
        for k in range(2):
            target = route[:, k:k + 1].astype(jnp.float32) * SLOTS + jnp.sum(ahead * hits[k], axis=1, keepdims=True)
            here = slot_ids == target
            mix = jnp.where(here, share[:, k:k + 1], mix)
            select = jnp.where(here, 1.0, select)
        high = mix.astype(jnp.bfloat16)
        low = (mix - high.astype(jnp.float32)).astype(jnp.bfloat16)
        return jnp.transpose(select).astype(jnp.bfloat16), high, low

    def saved_of(tick):
        second = jnp.broadcast_to(micro_is_second(tick), saved_ref.shape[1:])
        return jnp.where(second, saved_ref[1], saved_ref[0])

    def hop(number, slot, buffer, k):
        rows, cols = place(y, x, core)
        return pltpu.make_async_remote_copy(
            src_ref=sent.at[slot, slot_rows(*chip(k)), :], dst_ref=buffer.at[rows, cols],
            send_sem=hop_send.at[number, k - 1], recv_sem=hop_recv.at[number, k - 1],
            device_id=peer(k), device_id_type=pl.DeviceIdType.MESH)

    def to_twin(number, slot, buffer, k):
        rows, cols = place(*chip(k), core)
        source = sent.at[slot, slot_rows(y, x), :] if k == 0 else buffer.at[rows, cols]
        return pltpu.make_async_remote_copy(
            src_ref=source, dst_ref=buffer.at[rows, cols],
            send_sem=twin_send.at[number, k], recv_sem=twin_recv.at[number, k],
            device_id=twin, device_id_type=pl.DeviceIdType.MESH)

    def send_rows(number, slot, buffer, select, data):
        sent[slot] = jnp.dot(select, data, preferred_element_type=jnp.float32).astype(jnp.bfloat16)
        for k in (3, 1, 2):
            hop(number, slot, buffer, k).start()
        to_twin(number, slot, buffer, 0).start()
        rows, cols = place(y, x, core)
        buffer[rows, cols] = sent[slot, slot_rows(y, x), :]

    def relay_rows(number, slot, buffer):
        for k in (1, 2, 3):
            hop(number, slot, buffer, k).wait_recv()
            to_twin(number, slot, buffer, k).start()

    def finish_rows(number, slot, buffer):
        for k in range(4):
            to_twin(number, slot, buffer, k).wait_recv()
        for k in range(4):
            to_twin(number, slot, buffer, k).wait_send()
        for k in (1, 2, 3):
            hop(number, slot, buffer, k).wait_send()

    def factor_steps(tick, first, last):
        def body(i, carry):
            if tick == 0:
                up_copy(i).wait()
            cols = pl.ds(pl.multiple_of(i * HIDDEN_STEP, HIDDEN_STEP), HIDDEN_STEP)
            pre = jnp.dot(saved_rows[tick], up[:, cols], preferred_element_type=jnp.float32)
            sg = 1.0 / (1.0 + jnp.exp(-pre))
            factor[:, cols] = sg * (1.0 + pre * (1.0 - sg))
            return carry
        lax.fori_loop(first, last, body, 0)

    def pre_grad_steps(tick):
        def body(i, carry):
            if tick == 0:
                down_copy(i).wait()
            cols = pl.ds(pl.multiple_of(i * HIDDEN_STEP, HIDDEN_STEP), HIDDEN_STEP)
            act = lax.dot_general(grad_rows[...], down[cols, :], LAST_WITH_LAST, preferred_element_type=jnp.float32)
            pre_grad[:, cols] = (act * factor[:, cols]).astype(jnp.bfloat16)
            return carry
        lax.fori_loop(0, steps, body, 0)

    def branch_steps(quarter_id, store):
        def body(i, carry):
            start = pl.multiple_of(i * FEATURE_STEP, FEATURE_STEP)
            rows = pl.ds(pl.multiple_of(quarter_id * quarter + start, FEATURE_STEP), FEATURE_STEP)
            store(pl.ds(start, FEATURE_STEP),
                  lax.dot_general(pre_grad[...], up[rows, :], LAST_WITH_LAST, preferred_element_type=jnp.float32))
            return carry
        lax.fori_loop(0, quarter // FEATURE_STEP, body, 0)

    def part(tick, i):
        return pltpu.make_async_remote_copy(
            src_ref=part_out.at[i], dst_ref=part_in.at[i],
            send_sem=part_send.at[tick, i], recv_sem=part_recv.at[tick, i],
            device_id=twin, device_id_type=pl.DeviceIdType.MESH)

    def back(tick, k):
        py, _ = chip(k)
        return pltpu.make_async_remote_copy(
            src_ref=branch_out.at[k % 2, pl.ds(pl.multiple_of(py * SLOTS, SLOTS), SLOTS), :],
            dst_ref=arrived.at[slot_rows(y, x), :],
            send_sem=back_send.at[tick, k - 1], recv_sem=back_recv.at[tick, k - 1],
            device_id=peer(k), device_id_type=pl.DeviceIdType.MESH)

    def branches(tick):
        for i in (1, 0):
            px = lax.rem(x + i, 2)

            def store_out(cols, value, i=i):
                part_out[i, :, cols] = value

            branch_steps(px * 2 + 1 - core, store_out)
            part(tick, i).start()
        for i in (1, 0):
            px = lax.rem(x + i, 2)
            part(tick, i).wait_recv()

            def store_sum(cols, value, i=i):
                branch_out[i, :, cols] = (value + part_in[i, :, cols]).astype(jnp.bfloat16)

            branch_steps(px * 2 + core, store_sum)
            for k in ((3, 1) if i == 1 else (2,)):
                back(tick, k).start()
        arrived[slot_rows(y, x), :] = branch_out[0, pl.ds(pl.multiple_of(y * SLOTS, SLOTS), SLOTS), :]

    def combine(tick, current, high, low):
        for k in (3, 1, 2):
            back(tick, k).wait_recv()
        rows = arrived[...]
        moe = (jnp.dot(high, rows, preferred_element_type=jnp.float32)
               + jnp.dot(low, rows, preferred_element_type=jnp.float32))
        result[tick] = (current.astype(jnp.float32) + moe).astype(jnp.bfloat16)
        pass_on(tick).start()

    def finish_branches(tick):
        for i in range(2):
            part(tick, i).wait_send()
        for k in (1, 2, 3):
            back(tick, k).wait_send()

    def pass_on(tick):
        return pltpu.make_async_remote_copy(
            src_ref=result.at[tick], dst_ref=passed.at[tick],
            send_sem=pass_send.at[tick], recv_sem=pass_recv.at[tick],
            device_id=before, device_id_type=pl.DeviceIdType.MESH)

    select0, high0, low0 = routing(0)
    pl.semaphore_wait(barrier, len(partners))
    send_rows(0, 0, saved_rows.at[0], select0, saved_of(0))
    send_rows(1, 1, grad_rows, select0, grad_ref[...])
    relay_rows(0, 0, saved_rows.at[0])
    select1, high1, low1 = routing(1)
    finish_rows(0, 0, saved_rows.at[0])
    factor_steps(0, 0, steps)
    relay_rows(1, 1, grad_rows)
    send_rows(2, 2, saved_rows.at[1], select1, saved_of(1))
    finish_rows(1, 1, grad_rows)
    pre_grad_steps(0)
    relay_rows(2, 2, saved_rows.at[1])
    branches(0)
    finish_rows(2, 2, saved_rows.at[1])
    factor_steps(1, 0, steps // 4)
    combine(0, grad_ref[...], high0, low0)
    finish_branches(0)
    factor_steps(1, steps // 4, 3 * steps // 4)
    pass_on(0).wait()
    send_rows(3, 1, grad_rows, select1, passed[0])
    factor_steps(1, 3 * steps // 4, steps)
    relay_rows(3, 1, grad_rows)
    finish_rows(3, 1, grad_rows)
    pre_grad_steps(1)
    branches(1)
    combine(1, passed[0], high1, low1)
    finish_branches(1)
    pass_on(1).wait()
    out_ref[...] = passed[1]


def fused(grad_in, saved_input, routes, route_weights, plan, up_weight, down_weight):
    n_section = lax.axis_size("section")
    tokens, quarter = grad_in.shape[1:]
    width, hidden = up_weight.shape[1:]
    rows = 2 * SLOTS
    steps = hidden // HIDDEN_STEP
    vmem = pl.BlockSpec(memory_space=pltpu.VMEM)
    hbm = pl.BlockSpec(memory_space=pl.ANY)
    bf16, f32 = jnp.bfloat16, jnp.float32
    dma = pltpu.SemaphoreType.DMA
    flops = 2 * 2 * 3 * rows * width * hidden

    def body(*refs):
        fused_kernel(n_section, *refs)

    out = pl.pallas_call(
        body,
        out_shape=jax.ShapeDtypeStruct((tokens, quarter), bf16),
        in_specs=[vmem, vmem, vmem, vmem, vmem, hbm, hbm],
        out_specs=vmem,
        scratch_shapes=[
            pltpu.VMEM((width, hidden), bf16),
            pltpu.VMEM((hidden, width), bf16),
            pltpu.VMEM((2, rows, width), bf16),
            pltpu.VMEM((rows, width), bf16),
            pltpu.VMEM((rows, hidden), f32),
            pltpu.VMEM((rows, hidden), bf16),
            pltpu.VMEM((3, EXPERTS * SLOTS, quarter), bf16),
            pltpu.VMEM((2, rows, quarter), f32),
            pltpu.VMEM((2, rows, quarter), f32),
            pltpu.VMEM((2, rows, quarter), bf16),
            pltpu.VMEM((EXPERTS * SLOTS, quarter), bf16),
            pltpu.VMEM((2, tokens, quarter), bf16),
            pltpu.VMEM((2, tokens, quarter), bf16),
            dma((2, steps)),
            dma((4, 3)), dma((4, 3)),
            dma((4, 4)), dma((4, 4)),
            dma((2, 2)), dma((2, 2)),
            dma((2, 3)), dma((2, 3)),
            dma((2,)), dma((2,)),
        ],
        compiler_params=pltpu.CompilerParams(
            collective_id=0, has_side_effects=True, vmem_limit_bytes=VMEM_LIMIT),
        cost_estimate=pl.CostEstimate(flops=flops, bytes_accessed=4 * width * hidden, transcendentals=0),
    )(grad_in[0], saved_input[0], routes[0], route_weights[0], plan, up_weight, down_weight)
    return out[None]


VMEM_LIMIT = 64 * 1024 * 1024


def from_behind(value, axis, by):
    devices = lax.axis_size(axis)
    return lax.ppermute(value, axis, [(i, (i + by) % devices) for i in range(devices)])


def targets(route_now):
    expert_ids = jnp.arange(EXPERTS, dtype=jnp.int32)
    onehot = (route_now[:, :, None] == expert_ids[None, None, :]).astype(jnp.int32)
    counts = jnp.sum(onehot, axis=1)
    before = jnp.cumsum(counts, axis=0) - counts
    slot_pos = jnp.sum(before[:, None, :] * onehot, axis=2)
    return route_now * CAPACITY + slot_pos


def per_device(grad_in, saved_input, routes, route_weights, plan, up_weight, down_weight):
    n_expert = lax.axis_size("expert")
    n_mp = lax.axis_size("mp")
    split_size = n_expert * n_mp // EXPERTS
    quarter = grad_in.shape[2]
    width = quarter * n_mp
    up_local = up_weight[0]
    down_local = down_weight[0]
    slot_ids = jnp.arange(EXPERTS * CAPACITY, dtype=jnp.int32)
    contract_last = (((1,), (1,)), ((), ()))
    current = grad_in[0]
    for step_index in range(plan.shape[1]):
        micro_index = plan[0, step_index]
        saved_now = lax.dynamic_index_in_dim(saved_input[0], micro_index, 0, keepdims=False)
        route_now = lax.dynamic_index_in_dim(routes[0], micro_index, 0, keepdims=False)
        share_now = lax.dynamic_index_in_dim(route_weights[0], micro_index, 0, keepdims=False)
        target = targets(route_now)
        hit_mask = target[None, :, :] == slot_ids[:, None, None]
        select = jnp.any(hit_mask, axis=2).astype(jnp.bfloat16)
        saved_sent = (
            jnp.dot(select, saved_now, preferred_element_type=jnp.float32)
            .astype(jnp.bfloat16)
            .reshape(EXPERTS, CAPACITY, quarter)
        )
        grad_sent = (
            jnp.dot(select, current, preferred_element_type=jnp.float32)
            .astype(jnp.bfloat16)
            .reshape(EXPERTS, CAPACITY, quarter)
        )

        def copies(array):
            return jnp.broadcast_to(
                array[:, None], (EXPERTS, split_size, CAPACITY, quarter)
            ).reshape(EXPERTS * split_size, CAPACITY, quarter)

        saved_got, grad_got = (
            lax.all_to_all(
                copies(saved_sent), ("expert", "mp"), split_axis=0, concat_axis=0, tiled=True
            ),
            lax.all_to_all(
                copies(grad_sent), ("expert", "mp"), split_axis=0, concat_axis=0, tiled=True
            ),
        )

        def assemble(array):
            return (
                array.reshape(n_expert, n_mp, CAPACITY, quarter)
                .transpose(0, 2, 1, 3)
                .reshape(n_expert * CAPACITY, width)
            )

        saved_rows = assemble(saved_got)
        grad_rows = assemble(grad_got)
        upper_pre = jnp.dot(saved_rows, up_local, preferred_element_type=jnp.float32)
        grad_act = lax.dot_general(
            grad_rows, down_local, contract_last, preferred_element_type=jnp.float32
        )
        sigma_up = jax.nn.sigmoid(upper_pre)
        grad_pre = (grad_act * sigma_up * (1.0 + upper_pre * (1.0 - sigma_up))).astype(jnp.bfloat16)
        partial_rows = lax.dot_general(
            grad_pre, up_local, contract_last, preferred_element_type=jnp.float32
        )
        outgoing = (
            partial_rows.reshape(n_expert, CAPACITY, n_mp, quarter)
            .transpose(0, 2, 1, 3)
            .reshape(n_expert * n_mp, CAPACITY, quarter)
        )
        arrived = lax.all_to_all(
            outgoing, ("expert", "mp"), split_axis=0, concat_axis=0, tiled=True
        )
        summed = jnp.sum(arrived.reshape(EXPERTS, split_size, CAPACITY, quarter), axis=1)
        mixing = jnp.sum(jnp.where(hit_mask, share_now[None, :, :], 0.0), axis=2)
        moe_term = lax.dot_general(
            mixing,
            summed.reshape(EXPERTS * CAPACITY, quarter),
            (((0,), (0,)), ((), ())),
            precision=lax.Precision.HIGHEST,
            preferred_element_type=jnp.float32,
        )
        result = (current.astype(jnp.float32) + moe_term).astype(jnp.bfloat16)
        current = from_behind(result, "section", -1)
    return current[None]


def solution(mesh):
    small = (mesh.shape["expert"], mesh.shape["mp"]) == (2, 4) and mesh.shape["section"] > 2
    placed = (
        P("section", "expert", "mp"),
        P("section", None, "expert", "mp"),
        P("section", None, "expert", None),
        P("section", None, "expert", None),
        P("section", None),
        P("section", None, ("expert", "mp")),
        P("section", ("expert", "mp"), None),
    )
    return jax.shard_map(
        fused if small else per_device,
        mesh=mesh,
        in_specs=placed,
        out_specs=P("section", "expert", "mp"),
        check_vma=False,
    )
```

```python
import jax
import jax.numpy as jnp
from jax import lax
from jax.experimental import pallas as pl
from jax.experimental.pallas import tpu as pltpu
from jax.sharding import PartitionSpec as P

EXPERTS = 4
CAPACITY = 72
SLOTS = 80
HIDDEN_STEP = 512
FIRST_PIECE = 512
FEATURE_STEP = 256
LAST_WITH_LAST = (((1,), (1,)), ((), ()))


def fused_kernel(n_section, grad_ref, saved_ref, routes_ref, shares_ref, plan_ref, up_hbm, down_hbm, out_ref,
                 up, down, saved_rows, grad_rows, factor, pre_grad, sent, part_out, part_in, branch_out, arrived,
                 result, passed, weight_sem, hop_send, hop_recv, twin_send, twin_recv, part_send, part_recv,
                 back_send, back_recv, pass_send, pass_recv):
    section, y, mp = lax.axis_index("section"), lax.axis_index("expert"), lax.axis_index("mp")
    x, core = mp // 2, mp % 2
    quarter = grad_ref.shape[1]
    hidden = up.shape[1]
    steps = hidden // HIDDEN_STEP
    pieces = ((0, FIRST_PIECE), (FIRST_PIECE, quarter - FIRST_PIECE))
    twin = (section, y, x * 2 + 1 - core)
    before = (lax.rem(section + n_section - 1, n_section), y, mp)
    behind = (lax.rem(section + 1, n_section), y, mp)

    def chip(k):
        return lax.rem(y + k // 2, 2), lax.rem(x + k % 2, 2)

    def peer(k):
        py, px = chip(k)
        return (section, py, px * 2 + core)

    def place(py, px, pcore, p):
        first, size = pieces[p]
        return (pl.ds(pl.multiple_of(py * SLOTS, SLOTS), SLOTS),
                pl.ds(pl.multiple_of((px * 2 + pcore) * quarter + first, 256), size))

    def piece(p):
        return pl.ds(*pieces[p])

    def slot_rows(py, px):
        return pl.ds(pl.multiple_of((py * 2 + px) * SLOTS, SLOTS), SLOTS)

    def up_copy(i):
        cols = pl.ds(pl.multiple_of(i * HIDDEN_STEP, HIDDEN_STEP), HIDDEN_STEP)
        return pltpu.make_async_copy(up_hbm.at[0, :, cols], up.at[:, cols], weight_sem.at[0, i])

    def down_copy(i):
        rows = pl.ds(pl.multiple_of(i * HIDDEN_STEP, HIDDEN_STEP), HIDDEN_STEP)
        return pltpu.make_async_copy(down_hbm.at[0, rows, :], down.at[rows, :], weight_sem.at[1, i])

    def start_weights(i, carry):
        up_copy(i).start()
        return carry

    def start_weights_down(i, carry):
        down_copy(i).start()
        return carry

    lax.fori_loop(0, steps, start_weights, 0)

    barrier = pltpu.get_barrier_semaphore()
    partners = [twin, peer(1), peer(2), peer(3), before, behind]
    for partner in partners:
        pl.semaphore_signal(barrier, inc=1, device_id=partner, device_id_type=pl.DeviceIdType.MESH)

    tokens = routes_ref.shape[2]
    expert_ids = lax.broadcasted_iota(jnp.int32, (8, tokens), 0)
    earlier = (lax.broadcasted_iota(jnp.int32, (tokens, tokens), 0)
               < lax.broadcasted_iota(jnp.int32, (tokens, tokens), 1)).astype(jnp.float32).astype(jnp.bfloat16)
    slot_ids = lax.broadcasted_iota(jnp.int32, (EXPERTS * SLOTS, tokens), 0).astype(jnp.float32)

    def micro_is_second(tick):
        return plan_ref[0:1, tick:tick + 1] == 1

    def routing(tick):
        second = jnp.broadcast_to(micro_is_second(tick), (2, tokens))
        route = jnp.where(second, routes_ref[1], routes_ref[0])
        share = jnp.where(second, shares_ref[1], shares_ref[0])
        hits = [(expert_ids == route[k:k + 1, :]).astype(jnp.float32) for k in range(2)]
        counts = hits[0] + hits[1]
        ahead = jnp.dot(counts.astype(jnp.bfloat16), earlier, preferred_element_type=jnp.float32)
        mix = jnp.zeros((EXPERTS * SLOTS, tokens), jnp.float32)
        select = jnp.zeros((EXPERTS * SLOTS, tokens), jnp.float32)
        for k in range(2):
            target = route[k:k + 1, :].astype(jnp.float32) * SLOTS + jnp.sum(ahead * hits[k], axis=0, keepdims=True)
            here = slot_ids == target
            mix = jnp.where(here, share[k:k + 1, :], mix)
            select = jnp.where(here, 1.0, select)
        mix = jnp.transpose(mix)
        high = mix.astype(jnp.bfloat16)
        low = (mix - high.astype(jnp.float32)).astype(jnp.bfloat16)
        return select.astype(jnp.bfloat16), high, low

    def saved_of(tick):
        second = jnp.broadcast_to(micro_is_second(tick), saved_ref.shape[1:])
        return jnp.where(second, saved_ref[1], saved_ref[0])

    def hop(number, slot, buffer, p, k):
        rows, cols = place(y, x, core, p)
        return pltpu.make_async_remote_copy(
            src_ref=sent.at[slot, slot_rows(*chip(k)), piece(p)], dst_ref=buffer.at[rows, cols],
            send_sem=hop_send.at[number, p, k - 1], recv_sem=hop_recv.at[number, p, k - 1],
            device_id=peer(k), device_id_type=pl.DeviceIdType.MESH)

    def to_twin(number, slot, buffer, p, k):
        rows, cols = place(*chip(k), core, p)
        source = sent.at[slot, slot_rows(y, x), piece(p)] if k == 0 else buffer.at[rows, cols]
        return pltpu.make_async_remote_copy(
            src_ref=source, dst_ref=buffer.at[rows, cols],
            send_sem=twin_send.at[number, p, k], recv_sem=twin_recv.at[number, p, k],
            device_id=twin, device_id_type=pl.DeviceIdType.MESH)

    def send_rows(number, slot, buffer, p, select, data):
        sent[slot, :, piece(p)] = jnp.dot(select, data, preferred_element_type=jnp.float32).astype(jnp.bfloat16)
        for k in (3, 1, 2):
            hop(number, slot, buffer, p, k).start()
        to_twin(number, slot, buffer, p, 0).start()
        rows, cols = place(y, x, core, p)
        buffer[rows, cols] = sent[slot, slot_rows(y, x), piece(p)]

    def relay_rows(number, slot, buffer, p):
        for k in (2, 1, 3):
            hop(number, slot, buffer, p, k).wait_recv()
            to_twin(number, slot, buffer, p, k).start()

    def rows_there(number, slot, buffer):
        for p in range(2):
            for k in range(4):
                to_twin(number, slot, buffer, p, k).wait_recv()

    def rows_gone(number, slot, buffer):
        for p in range(2):
            for k in range(4):
                to_twin(number, slot, buffer, p, k).wait_send()
            for k in (1, 2, 3):
                hop(number, slot, buffer, p, k).wait_send()

    def factor_steps(tick, first, last):
        def body(i, carry):
            if tick == 0:
                up_copy(i).wait()
            cols = pl.ds(pl.multiple_of(i * HIDDEN_STEP, HIDDEN_STEP), HIDDEN_STEP)
            pre = jnp.dot(saved_rows[tick], up[:, cols], preferred_element_type=jnp.float32)
            sg = 1.0 / (1.0 + jnp.exp(-pre))
            factor[:, cols] = sg * (1.0 + pre * (1.0 - sg))
            return carry
        lax.fori_loop(first, last, body, 0)

    def pre_grad_steps(tick):
        def body(i, carry):
            if tick == 0:
                down_copy(i).wait()
            cols = pl.ds(pl.multiple_of(i * HIDDEN_STEP, HIDDEN_STEP), HIDDEN_STEP)
            act = lax.dot_general(grad_rows[...], down[cols, :], LAST_WITH_LAST, preferred_element_type=jnp.float32)
            pre_grad[:, cols] = (act * factor[:, cols]).astype(jnp.bfloat16)
            return carry
        lax.fori_loop(0, hidden // HIDDEN_STEP, body, 0)

    def branch_steps(quarter_id, first, size, store):
        def body(i, carry):
            start = pl.multiple_of(first + i * FEATURE_STEP, FEATURE_STEP)
            rows = pl.ds(pl.multiple_of(quarter_id * quarter + start, FEATURE_STEP), FEATURE_STEP)
            store(pl.ds(start, FEATURE_STEP),
                  lax.dot_general(pre_grad[...], up[rows, :], LAST_WITH_LAST, preferred_element_type=jnp.float32))
            return carry
        lax.fori_loop(0, size // FEATURE_STEP, body, 0)

    def part(tick, i):
        return pltpu.make_async_remote_copy(
            src_ref=part_out.at[i], dst_ref=part_in.at[i],
            send_sem=part_send.at[tick, i], recv_sem=part_recv.at[tick, i],
            device_id=twin, device_id_type=pl.DeviceIdType.MESH)

    def back(tick, p, k):
        py, _ = chip(k)
        return pltpu.make_async_remote_copy(
            src_ref=branch_out.at[k % 2, pl.ds(pl.multiple_of(py * SLOTS, SLOTS), SLOTS), piece(p)],
            dst_ref=arrived.at[slot_rows(y, x), piece(p)],
            send_sem=back_send.at[tick, p, k - 1], recv_sem=back_recv.at[tick, p, k - 1],
            device_id=peer(k), device_id_type=pl.DeviceIdType.MESH)

    def branches(tick):
        for i in (1, 0):
            px = lax.rem(x + i, 2)

            def store_out(cols, value, i=i):
                part_out[i, :, cols] = value

            branch_steps(px * 2 + 1 - core, 0, quarter, store_out)
            part(tick, i).start()
        for p in range(2):
            for i in (1, 0):
                px = lax.rem(x + i, 2)
                if p == 0:
                    part(tick, i).wait_recv()

                def store_sum(cols, value, i=i):
                    branch_out[i, :, cols] = (value + part_in[i, :, cols]).astype(jnp.bfloat16)

                branch_steps(px * 2 + core, *pieces[p], store_sum)
                for k in ((3, 1) if i == 1 else (2,)):
                    back(tick, p, k).start()
            arrived[slot_rows(y, x), piece(p)] = branch_out[0, pl.ds(pl.multiple_of(y * SLOTS, SLOTS), SLOTS), piece(p)]

    def combine(tick, p, current, high, low):
        for k in (2, 1, 3):
            back(tick, p, k).wait_recv()
        rows = arrived[:, piece(p)]
        moe = (jnp.dot(high, rows, preferred_element_type=jnp.float32)
               + jnp.dot(low, rows, preferred_element_type=jnp.float32))
        result[tick, :, piece(p)] = (current.astype(jnp.float32) + moe).astype(jnp.bfloat16)
        pass_on(tick, p).start()

    def finish_branches(tick):
        for i in range(2):
            part(tick, i).wait_send()
        for p in range(2):
            for k in (1, 2, 3):
                back(tick, p, k).wait_send()

    def pass_on(tick, p):
        return pltpu.make_async_remote_copy(
            src_ref=result.at[tick, :, piece(p)], dst_ref=passed.at[tick, :, piece(p)],
            send_sem=pass_send.at[tick, p], recv_sem=pass_recv.at[tick, p],
            device_id=before, device_id_type=pl.DeviceIdType.MESH)

    select0, high0, low0 = routing(0)
    pl.semaphore_wait(barrier, len(partners))
    saved0, saved1 = saved_rows.at[0], saved_rows.at[1]
    rows_of = saved_of(0)
    for p in range(2):
        first, size = pieces[p]
        send_rows(0, 0, saved0, p, select0, rows_of[:, first:first + size])
    for p in range(2):
        relay_rows(0, 0, saved0, p)
    lax.fori_loop(0, steps, start_weights_down, 0)
    for p in range(2):
        send_rows(1, 1, grad_rows, p, select0, grad_ref[:, piece(p)])
    rows_there(0, 0, saved0)
    factor_steps(0, 0, steps)
    for p in range(2):
        relay_rows(1, 1, grad_rows, p)
    select1, high1, low1 = routing(1)
    rows_gone(0, 0, saved0)
    rows_of = saved_of(1)
    for p in range(2):
        first, size = pieces[p]
        send_rows(2, 0, saved1, p, select1, rows_of[:, first:first + size])
    rows_there(1, 1, grad_rows)
    pre_grad_steps(0)
    for p in range(2):
        relay_rows(2, 0, saved1, p)
    rows_gone(1, 1, grad_rows)
    branches(0)
    rows_there(2, 0, saved1)
    combine(0, 0, grad_ref[:, piece(0)], high0, low0)
    factor_steps(1, 0, 1)
    combine(0, 1, grad_ref[:, piece(1)], high0, low0)
    factor_steps(1, 1, 4)
    pass_on(0, 0).wait_recv()
    send_rows(3, 1, grad_rows, 0, select1, passed[0, :, piece(0)])
    factor_steps(1, 4, 5)
    pass_on(0, 1).wait_recv()
    send_rows(3, 1, grad_rows, 1, select1, passed[0, :, piece(1)])
    factor_steps(1, 5, 6)
    relay_rows(3, 1, grad_rows, 0)
    factor_steps(1, 6, steps)
    relay_rows(3, 1, grad_rows, 1)
    finish_branches(0)
    rows_gone(2, 0, saved1)
    rows_there(3, 1, grad_rows)
    pre_grad_steps(1)
    branches(1)
    for p in range(2):
        combine(1, p, passed[0, :, piece(p)], high1, low1)
    rows_gone(3, 1, grad_rows)
    finish_branches(1)
    for p in range(2):
        pass_on(0, p).wait_send()
        pass_on(1, p).wait()
    out_ref[...] = passed[1]


def fused(grad_in, saved_input, routes, route_weights, plan, up_weight, down_weight):
    n_section = lax.axis_size("section")
    tokens, quarter = grad_in.shape[1:]
    width, hidden = up_weight.shape[1:]
    rows = 2 * SLOTS
    steps = hidden // HIDDEN_STEP
    vmem = pl.BlockSpec(memory_space=pltpu.VMEM)
    hbm = pl.BlockSpec(memory_space=pl.ANY)
    bf16, f32 = jnp.bfloat16, jnp.float32
    dma = pltpu.SemaphoreType.DMA
    flops = 2 * 2 * 3 * rows * width * hidden

    def body(*refs):
        fused_kernel(n_section, *refs)

    out = pl.pallas_call(
        body,
        out_shape=jax.ShapeDtypeStruct((tokens, quarter), bf16),
        in_specs=[vmem, vmem, vmem, vmem, vmem, hbm, hbm],
        out_specs=vmem,
        scratch_shapes=[
            pltpu.VMEM((width, hidden), bf16),
            pltpu.VMEM((hidden, width), bf16),
            pltpu.VMEM((2, rows, width), bf16),
            pltpu.VMEM((rows, width), bf16),
            pltpu.VMEM((rows, hidden), f32),
            pltpu.VMEM((rows, hidden), bf16),
            pltpu.VMEM((2, EXPERTS * SLOTS, quarter), bf16),
            pltpu.VMEM((2, rows, quarter), f32),
            pltpu.VMEM((2, rows, quarter), f32),
            pltpu.VMEM((2, rows, quarter), bf16),
            pltpu.VMEM((EXPERTS * SLOTS, quarter), bf16),
            pltpu.VMEM((2, tokens, quarter), bf16),
            pltpu.VMEM((2, tokens, quarter), bf16),
            dma((2, steps)),
            dma((4, 2, 3)), dma((4, 2, 3)),
            dma((4, 2, 4)), dma((4, 2, 4)),
            dma((2, 2)), dma((2, 2)),
            dma((2, 2, 3)), dma((2, 2, 3)),
            dma((2, 2)), dma((2, 2)),
        ],
        compiler_params=pltpu.CompilerParams(
            collective_id=0, has_side_effects=True, vmem_limit_bytes=VMEM_LIMIT),
        cost_estimate=pl.CostEstimate(flops=flops, bytes_accessed=4 * width * hidden, transcendentals=0),
    )(grad_in[0], saved_input[0], routes[0].transpose(0, 2, 1), route_weights[0].transpose(0, 2, 1), plan, up_weight, down_weight)
    return out[None]


VMEM_LIMIT = 64 * 1024 * 1024


def from_behind(value, axis, by):
    devices = lax.axis_size(axis)
    return lax.ppermute(value, axis, [(i, (i + by) % devices) for i in range(devices)])


def targets(route_now):
    expert_ids = jnp.arange(EXPERTS, dtype=jnp.int32)
    onehot = (route_now[:, :, None] == expert_ids[None, None, :]).astype(jnp.int32)
    counts = jnp.sum(onehot, axis=1)
    before = jnp.cumsum(counts, axis=0) - counts
    slot_pos = jnp.sum(before[:, None, :] * onehot, axis=2)
    return route_now * CAPACITY + slot_pos


def per_device(grad_in, saved_input, routes, route_weights, plan, up_weight, down_weight):
    n_expert = lax.axis_size("expert")
    n_mp = lax.axis_size("mp")
    split_size = n_expert * n_mp // EXPERTS
    quarter = grad_in.shape[2]
    width = quarter * n_mp
    up_local = up_weight[0]
    down_local = down_weight[0]
    slot_ids = jnp.arange(EXPERTS * CAPACITY, dtype=jnp.int32)
    contract_last = (((1,), (1,)), ((), ()))
    current = grad_in[0]
    for step_index in range(plan.shape[1]):
        micro_index = plan[0, step_index]
        saved_now = lax.dynamic_index_in_dim(saved_input[0], micro_index, 0, keepdims=False)
        route_now = lax.dynamic_index_in_dim(routes[0], micro_index, 0, keepdims=False)
        share_now = lax.dynamic_index_in_dim(route_weights[0], micro_index, 0, keepdims=False)
        target = targets(route_now)
        hit_mask = target[None, :, :] == slot_ids[:, None, None]
        select = jnp.any(hit_mask, axis=2).astype(jnp.bfloat16)
        saved_sent = (
            jnp.dot(select, saved_now, preferred_element_type=jnp.float32)
            .astype(jnp.bfloat16)
            .reshape(EXPERTS, CAPACITY, quarter)
        )
        grad_sent = (
            jnp.dot(select, current, preferred_element_type=jnp.float32)
            .astype(jnp.bfloat16)
            .reshape(EXPERTS, CAPACITY, quarter)
        )

        def copies(array):
            return jnp.broadcast_to(
                array[:, None], (EXPERTS, split_size, CAPACITY, quarter)
            ).reshape(EXPERTS * split_size, CAPACITY, quarter)

        saved_got, grad_got = (
            lax.all_to_all(
                copies(saved_sent), ("expert", "mp"), split_axis=0, concat_axis=0, tiled=True
            ),
            lax.all_to_all(
                copies(grad_sent), ("expert", "mp"), split_axis=0, concat_axis=0, tiled=True
            ),
        )

        def assemble(array):
            return (
                array.reshape(n_expert, n_mp, CAPACITY, quarter)
                .transpose(0, 2, 1, 3)
                .reshape(n_expert * CAPACITY, width)
            )

        saved_rows = assemble(saved_got)
        grad_rows = assemble(grad_got)
        upper_pre = jnp.dot(saved_rows, up_local, preferred_element_type=jnp.float32)
        grad_act = lax.dot_general(
            grad_rows, down_local, contract_last, preferred_element_type=jnp.float32
        )
        sigma_up = jax.nn.sigmoid(upper_pre)
        grad_pre = (grad_act * sigma_up * (1.0 + upper_pre * (1.0 - sigma_up))).astype(jnp.bfloat16)
        partial_rows = lax.dot_general(
            grad_pre, up_local, contract_last, preferred_element_type=jnp.float32
        )
        outgoing = (
            partial_rows.reshape(n_expert, CAPACITY, n_mp, quarter)
            .transpose(0, 2, 1, 3)
            .reshape(n_expert * n_mp, CAPACITY, quarter)
        )
        arrived = lax.all_to_all(
            outgoing, ("expert", "mp"), split_axis=0, concat_axis=0, tiled=True
        )
        summed = jnp.sum(arrived.reshape(EXPERTS, split_size, CAPACITY, quarter), axis=1)
        mixing = jnp.sum(jnp.where(hit_mask, share_now[None, :, :], 0.0), axis=2)
        moe_term = lax.dot_general(
            mixing,
            summed.reshape(EXPERTS * CAPACITY, quarter),
            (((0,), (0,)), ((), ())),
            precision=lax.Precision.HIGHEST,
            preferred_element_type=jnp.float32,
        )
        result = (current.astype(jnp.float32) + moe_term).astype(jnp.bfloat16)
        current = from_behind(result, "section", -1)
    return current[None]


def solution(mesh):
    small = (mesh.shape["expert"], mesh.shape["mp"]) == (2, 4) and mesh.shape["section"] > 2
    placed = (
        P("section", "expert", "mp"),
        P("section", None, "expert", "mp"),
        P("section", None, "expert", None),
        P("section", None, "expert", None),
        P("section", None),
        P("section", None, ("expert", "mp")),
        P("section", ("expert", "mp"), None),
    )
    return jax.shard_map(
        fused if small else per_device,
        mesh=mesh,
        in_specs=placed,
        out_specs=P("section", "expert", "mp"),
        check_vma=False,
    )
```

```python
import jax
import jax.numpy as jnp
from jax import lax
from jax.experimental import pallas as pl
from jax.experimental.pallas import tpu as pltpu
from jax.sharding import PartitionSpec as P

EXPERTS = 4
CAPACITY = 72
SLOTS = 80
HIDDEN_STEP = 512
FIRST_PIECE = 512
LAST_WITH_LAST = (((1,), (1,)), ((), ()))


def fused_kernel(n_section, grad_ref, saved_ref, routes_ref, shares_ref, plan_ref, up_hbm, down_hbm, out_ref,
                 up, down, saved_rows, grad_rows, factor, pre_grad, sent, part_out, part_in, branch_out, arrived,
                 result, passed, weight_sem, hop_send, hop_recv, twin_send, twin_recv, part_send, part_recv,
                 back_send, back_recv, pass_send, pass_recv):
    section, y, mp = lax.axis_index("section"), lax.axis_index("expert"), lax.axis_index("mp")
    x, core = mp // 2, mp % 2
    quarter = grad_ref.shape[1]
    hidden = up.shape[1]
    steps = hidden // HIDDEN_STEP
    pieces = ((0, FIRST_PIECE), (FIRST_PIECE, quarter - FIRST_PIECE))
    twin = (section, y, x * 2 + 1 - core)
    before = (lax.rem(section + n_section - 1, n_section), y, mp)
    behind = (lax.rem(section + 1, n_section), y, mp)

    def chip(k):
        return lax.rem(y + k // 2, 2), lax.rem(x + k % 2, 2)

    def peer(k):
        py, px = chip(k)
        return (section, py, px * 2 + core)

    def place(py, px, pcore, p):
        first, size = pieces[p]
        return (pl.ds(pl.multiple_of(py * SLOTS, SLOTS), SLOTS),
                pl.ds(pl.multiple_of((px * 2 + pcore) * quarter + first, 256), size))

    def piece(p):
        return pl.ds(*pieces[p])

    def slot_rows(py, px):
        return pl.ds(pl.multiple_of((py * 2 + px) * SLOTS, SLOTS), SLOTS)

    def up_copy(i):
        cols = pl.ds(pl.multiple_of(i * HIDDEN_STEP, HIDDEN_STEP), HIDDEN_STEP)
        return pltpu.make_async_copy(up_hbm.at[0, :, cols], up.at[:, cols], weight_sem.at[0, i])

    def down_copy(i):
        rows = pl.ds(pl.multiple_of(i * HIDDEN_STEP, HIDDEN_STEP), HIDDEN_STEP)
        return pltpu.make_async_copy(down_hbm.at[0, rows, :], down.at[rows, :], weight_sem.at[1, i])

    def start_weights(i, carry):
        up_copy(i).start()
        return carry

    def start_weights_down(i, carry):
        down_copy(i).start()
        return carry

    lax.fori_loop(0, steps, start_weights, 0)

    barrier = pltpu.get_barrier_semaphore()
    partners = [twin, peer(1), peer(2), peer(3), before, behind]
    for partner in partners:
        pl.semaphore_signal(barrier, inc=1, device_id=partner, device_id_type=pl.DeviceIdType.MESH)

    tokens = routes_ref.shape[2]
    expert_ids = lax.broadcasted_iota(jnp.int32, (8, tokens), 0)
    earlier = (lax.broadcasted_iota(jnp.int32, (tokens, tokens), 0)
               < lax.broadcasted_iota(jnp.int32, (tokens, tokens), 1)).astype(jnp.float32).astype(jnp.bfloat16)
    slot_ids = lax.broadcasted_iota(jnp.int32, (EXPERTS * SLOTS, tokens), 0).astype(jnp.float32)

    def micro_is_second(tick):
        return plan_ref[0:1, tick:tick + 1] == 1

    def routing(tick):
        second = jnp.broadcast_to(micro_is_second(tick), (2, tokens))
        route = jnp.where(second, routes_ref[1], routes_ref[0])
        share = jnp.where(second, shares_ref[1], shares_ref[0])
        hits = [(expert_ids == route[k:k + 1, :]).astype(jnp.float32) for k in range(2)]
        counts = hits[0] + hits[1]
        ahead = jnp.dot(counts.astype(jnp.bfloat16), earlier, preferred_element_type=jnp.float32)
        mix = jnp.zeros((EXPERTS * SLOTS, tokens), jnp.float32)
        select = jnp.zeros((EXPERTS * SLOTS, tokens), jnp.float32)
        for k in range(2):
            target = route[k:k + 1, :].astype(jnp.float32) * SLOTS + jnp.sum(ahead * hits[k], axis=0, keepdims=True)
            here = slot_ids == target
            mix = jnp.where(here, share[k:k + 1, :], mix)
            select = jnp.where(here, 1.0, select)
        mix = jnp.transpose(mix)
        high = mix.astype(jnp.bfloat16)
        low = (mix - high.astype(jnp.float32)).astype(jnp.bfloat16)
        return select.astype(jnp.bfloat16), high, low

    def saved_of(tick):
        second = jnp.broadcast_to(micro_is_second(tick), saved_ref.shape[1:])
        return jnp.where(second, saved_ref[1], saved_ref[0])

    def hop(number, slot, buffer, p, k):
        rows, cols = place(y, x, core, p)
        return pltpu.make_async_remote_copy(
            src_ref=sent.at[slot, slot_rows(*chip(k)), piece(p)], dst_ref=buffer.at[rows, cols],
            send_sem=hop_send.at[number, p, k - 1], recv_sem=hop_recv.at[number, p, k - 1],
            device_id=peer(k), device_id_type=pl.DeviceIdType.MESH)

    def to_twin(number, slot, buffer, p, k):
        rows, cols = place(*chip(k), core, p)
        source = sent.at[slot, slot_rows(y, x), piece(p)] if k == 0 else buffer.at[rows, cols]
        return pltpu.make_async_remote_copy(
            src_ref=source, dst_ref=buffer.at[rows, cols],
            send_sem=twin_send.at[number, p, k], recv_sem=twin_recv.at[number, p, k],
            device_id=twin, device_id_type=pl.DeviceIdType.MESH)

    def send_rows(number, slot, buffer, p, select, data):
        sent[slot, :, piece(p)] = jnp.dot(select, data, preferred_element_type=jnp.float32).astype(jnp.bfloat16)
        for k in (3, 1, 2):
            hop(number, slot, buffer, p, k).start()
        to_twin(number, slot, buffer, p, 0).start()
        rows, cols = place(y, x, core, p)
        buffer[rows, cols] = sent[slot, slot_rows(y, x), piece(p)]

    def relay_rows(number, slot, buffer, p):
        for k in (2, 1, 3):
            hop(number, slot, buffer, p, k).wait_recv()
            to_twin(number, slot, buffer, p, k).start()

    def rows_there(number, slot, buffer):
        for p in range(2):
            for k in range(4):
                to_twin(number, slot, buffer, p, k).wait_recv()

    def rows_gone(number, slot, buffer):
        for p in range(2):
            for k in range(4):
                to_twin(number, slot, buffer, p, k).wait_send()
            for k in (1, 2, 3):
                hop(number, slot, buffer, p, k).wait_send()

    def factor_steps(tick, first, last):
        def body(i, carry):
            if tick == 0:
                up_copy(i).wait()
            cols = pl.ds(pl.multiple_of(i * HIDDEN_STEP, HIDDEN_STEP), HIDDEN_STEP)
            pre = jnp.dot(saved_rows[tick], up[:, cols], preferred_element_type=jnp.float32)
            sg = 1.0 / (1.0 + jnp.exp(-pre))
            factor[:, cols] = sg * (1.0 + pre * (1.0 - sg))
            return carry
        lax.fori_loop(first, last, body, 0)

    def pre_grad_steps(tick):
        def body(i, carry):
            if tick == 0:
                down_copy(i).wait()
            cols = pl.ds(pl.multiple_of(i * HIDDEN_STEP, HIDDEN_STEP), HIDDEN_STEP)
            act = lax.dot_general(grad_rows[...], down[cols, :], LAST_WITH_LAST, preferred_element_type=jnp.float32)
            pre_grad[:, cols] = (act * factor[:, cols]).astype(jnp.bfloat16)
            return carry
        lax.fori_loop(0, hidden // HIDDEN_STEP, body, 0, unroll=1 if tick == 0 else 2)

    def branch_of(quarter_id, p):
        first, size = pieces[p]
        rows = pl.ds(pl.multiple_of(quarter_id * quarter + first, 256), size)
        return lax.dot_general(pre_grad[...], up[rows, :], LAST_WITH_LAST, preferred_element_type=jnp.float32)

    def part(tick, i):
        return pltpu.make_async_remote_copy(
            src_ref=part_out.at[i], dst_ref=part_in.at[i],
            send_sem=part_send.at[tick, i], recv_sem=part_recv.at[tick, i],
            device_id=twin, device_id_type=pl.DeviceIdType.MESH)

    def back(tick, p, k):
        py, _ = chip(k)
        return pltpu.make_async_remote_copy(
            src_ref=branch_out.at[k % 2, pl.ds(pl.multiple_of(py * SLOTS, SLOTS), SLOTS), piece(p)],
            dst_ref=arrived.at[slot_rows(y, x), piece(p)],
            send_sem=back_send.at[tick, p, k - 1], recv_sem=back_recv.at[tick, p, k - 1],
            device_id=peer(k), device_id_type=pl.DeviceIdType.MESH)

    def branches(tick):
        for i in (1, 0):
            px = lax.rem(x + i, 2)
            for p in range(2):
                part_out[i, :, piece(p)] = branch_of(px * 2 + 1 - core, p).astype(jnp.bfloat16)
            part(tick, i).start()
        for p in range(2):
            for i in (1, 0):
                px = lax.rem(x + i, 2)
                if p == 0:
                    part(tick, i).wait_recv()
                own = branch_of(px * 2 + core, p) + part_in[i, :, piece(p)].astype(jnp.float32)
                branch_out[i, :, piece(p)] = own.astype(jnp.bfloat16)
                for k in ((3, 1) if i == 1 else (2,)):
                    back(tick, p, k).start()
            arrived[slot_rows(y, x), piece(p)] = branch_out[0, pl.ds(pl.multiple_of(y * SLOTS, SLOTS), SLOTS), piece(p)]

    def combine(tick, p, current, high, low):
        for k in (2, 1, 3):
            back(tick, p, k).wait_recv()
        rows = arrived[:, piece(p)]
        moe = (jnp.dot(high, rows, preferred_element_type=jnp.float32)
               + jnp.dot(low, rows, preferred_element_type=jnp.float32))
        result[tick, :, piece(p)] = (current.astype(jnp.float32) + moe).astype(jnp.bfloat16)
        pass_on(tick, p).start()

    def finish_branches(tick):
        for i in range(2):
            part(tick, i).wait_send()
        for p in range(2):
            for k in (1, 2, 3):
                back(tick, p, k).wait_send()

    def pass_on(tick, p):
        return pltpu.make_async_remote_copy(
            src_ref=result.at[tick, :, piece(p)], dst_ref=passed.at[tick, :, piece(p)],
            send_sem=pass_send.at[tick, p], recv_sem=pass_recv.at[tick, p],
            device_id=before, device_id_type=pl.DeviceIdType.MESH)

    select0, high0, low0 = routing(0)
    pl.semaphore_wait(barrier, len(partners))
    saved0, saved1 = saved_rows.at[0], saved_rows.at[1]
    rows_of = saved_of(0)
    for p in range(2):
        first, size = pieces[p]
        send_rows(0, 0, saved0, p, select0, rows_of[:, first:first + size])
    for p in range(2):
        relay_rows(0, 0, saved0, p)
    lax.fori_loop(0, steps, start_weights_down, 0)
    for p in range(2):
        send_rows(1, 1, grad_rows, p, select0, grad_ref[:, piece(p)])
    rows_there(0, 0, saved0)
    factor_steps(0, 0, steps)
    for p in range(2):
        relay_rows(1, 1, grad_rows, p)
    select1, high1, low1 = routing(1)
    rows_gone(0, 0, saved0)
    rows_of = saved_of(1)
    for p in range(2):
        first, size = pieces[p]
        send_rows(2, 0, saved1, p, select1, rows_of[:, first:first + size])
    rows_there(1, 1, grad_rows)
    pre_grad_steps(0)
    for p in range(2):
        relay_rows(2, 0, saved1, p)
    rows_gone(1, 1, grad_rows)
    branches(0)
    rows_there(2, 0, saved1)
    combine(0, 0, grad_ref[:, piece(0)], high0, low0)
    factor_steps(1, 0, 1)
    combine(0, 1, grad_ref[:, piece(1)], high0, low0)
    factor_steps(1, 1, 4)
    pass_on(0, 0).wait_recv()
    send_rows(3, 1, grad_rows, 0, select1, passed[0, :, piece(0)])
    factor_steps(1, 4, 5)
    pass_on(0, 1).wait_recv()
    send_rows(3, 1, grad_rows, 1, select1, passed[0, :, piece(1)])
    factor_steps(1, 5, 6)
    relay_rows(3, 1, grad_rows, 0)
    factor_steps(1, 6, steps)
    relay_rows(3, 1, grad_rows, 1)
    finish_branches(0)
    rows_gone(2, 0, saved1)
    rows_there(3, 1, grad_rows)
    pre_grad_steps(1)
    branches(1)
    for p in range(2):
        combine(1, p, passed[0, :, piece(p)], high1, low1)
    rows_gone(3, 1, grad_rows)
    finish_branches(1)
    for p in range(2):
        pass_on(0, p).wait_send()
        pass_on(1, p).wait()
    out_ref[...] = passed[1]


def fused(grad_in, saved_input, routes, route_weights, plan, up_weight, down_weight):
    n_section = lax.axis_size("section")
    tokens, quarter = grad_in.shape[1:]
    width, hidden = up_weight.shape[1:]
    rows = 2 * SLOTS
    steps = hidden // HIDDEN_STEP
    vmem = pl.BlockSpec(memory_space=pltpu.VMEM)
    hbm = pl.BlockSpec(memory_space=pl.ANY)
    bf16, f32 = jnp.bfloat16, jnp.float32
    dma = pltpu.SemaphoreType.DMA
    flops = 2 * 2 * 3 * rows * width * hidden

    def body(*refs):
        fused_kernel(n_section, *refs)

    out = pl.pallas_call(
        body,
        out_shape=jax.ShapeDtypeStruct((tokens, quarter), bf16),
        in_specs=[vmem, vmem, vmem, vmem, vmem, hbm, hbm],
        out_specs=vmem,
        scratch_shapes=[
            pltpu.VMEM((width, hidden), bf16),
            pltpu.VMEM((hidden, width), bf16),
            pltpu.VMEM((2, rows, width), bf16),
            pltpu.VMEM((rows, width), bf16),
            pltpu.VMEM((rows, hidden), f32),
            pltpu.VMEM((rows, hidden), bf16),
            pltpu.VMEM((2, EXPERTS * SLOTS, quarter), bf16),
            pltpu.VMEM((2, rows, quarter), bf16),
            pltpu.VMEM((2, rows, quarter), bf16),
            pltpu.VMEM((2, rows, quarter), bf16),
            pltpu.VMEM((EXPERTS * SLOTS, quarter), bf16),
            pltpu.VMEM((2, tokens, quarter), bf16),
            pltpu.VMEM((2, tokens, quarter), bf16),
            dma((2, steps)),
            dma((4, 2, 3)), dma((4, 2, 3)),
            dma((4, 2, 4)), dma((4, 2, 4)),
            dma((2, 2)), dma((2, 2)),
            dma((2, 2, 3)), dma((2, 2, 3)),
            dma((2, 2)), dma((2, 2)),
        ],
        compiler_params=pltpu.CompilerParams(
            collective_id=0, has_side_effects=True, vmem_limit_bytes=VMEM_LIMIT),
        cost_estimate=pl.CostEstimate(flops=flops, bytes_accessed=4 * width * hidden, transcendentals=0),
    )(grad_in[0], saved_input[0], routes[0].transpose(0, 2, 1), route_weights[0].transpose(0, 2, 1), plan, up_weight, down_weight)
    return out[None]


VMEM_LIMIT = 64 * 1024 * 1024


def from_behind(value, axis, by):
    devices = lax.axis_size(axis)
    return lax.ppermute(value, axis, [(i, (i + by) % devices) for i in range(devices)])


def targets(route_now):
    expert_ids = jnp.arange(EXPERTS, dtype=jnp.int32)
    onehot = (route_now[:, :, None] == expert_ids[None, None, :]).astype(jnp.int32)
    counts = jnp.sum(onehot, axis=1)
    before = jnp.cumsum(counts, axis=0) - counts
    slot_pos = jnp.sum(before[:, None, :] * onehot, axis=2)
    return route_now * CAPACITY + slot_pos


def per_device(grad_in, saved_input, routes, route_weights, plan, up_weight, down_weight):
    n_expert = lax.axis_size("expert")
    n_mp = lax.axis_size("mp")
    split_size = n_expert * n_mp // EXPERTS
    quarter = grad_in.shape[2]
    width = quarter * n_mp
    up_local = up_weight[0]
    down_local = down_weight[0]
    slot_ids = jnp.arange(EXPERTS * CAPACITY, dtype=jnp.int32)
    contract_last = (((1,), (1,)), ((), ()))
    current = grad_in[0]
    for step_index in range(plan.shape[1]):
        micro_index = plan[0, step_index]
        saved_now = lax.dynamic_index_in_dim(saved_input[0], micro_index, 0, keepdims=False)
        route_now = lax.dynamic_index_in_dim(routes[0], micro_index, 0, keepdims=False)
        share_now = lax.dynamic_index_in_dim(route_weights[0], micro_index, 0, keepdims=False)
        target = targets(route_now)
        hit_mask = target[None, :, :] == slot_ids[:, None, None]
        select = jnp.any(hit_mask, axis=2).astype(jnp.bfloat16)
        saved_sent = (
            jnp.dot(select, saved_now, preferred_element_type=jnp.float32)
            .astype(jnp.bfloat16)
            .reshape(EXPERTS, CAPACITY, quarter)
        )
        grad_sent = (
            jnp.dot(select, current, preferred_element_type=jnp.float32)
            .astype(jnp.bfloat16)
            .reshape(EXPERTS, CAPACITY, quarter)
        )

        def copies(array):
            return jnp.broadcast_to(
                array[:, None], (EXPERTS, split_size, CAPACITY, quarter)
            ).reshape(EXPERTS * split_size, CAPACITY, quarter)

        saved_got, grad_got = (
            lax.all_to_all(
                copies(saved_sent), ("expert", "mp"), split_axis=0, concat_axis=0, tiled=True
            ),
            lax.all_to_all(
                copies(grad_sent), ("expert", "mp"), split_axis=0, concat_axis=0, tiled=True
            ),
        )

        def assemble(array):
            return (
                array.reshape(n_expert, n_mp, CAPACITY, quarter)
                .transpose(0, 2, 1, 3)
                .reshape(n_expert * CAPACITY, width)
            )

        saved_rows = assemble(saved_got)
        grad_rows = assemble(grad_got)
        upper_pre = jnp.dot(saved_rows, up_local, preferred_element_type=jnp.float32)
        grad_act = lax.dot_general(
            grad_rows, down_local, contract_last, preferred_element_type=jnp.float32
        )
        sigma_up = jax.nn.sigmoid(upper_pre)
        grad_pre = (grad_act * sigma_up * (1.0 + upper_pre * (1.0 - sigma_up))).astype(jnp.bfloat16)
        partial_rows = lax.dot_general(
            grad_pre, up_local, contract_last, preferred_element_type=jnp.float32
        )
        outgoing = (
            partial_rows.reshape(n_expert, CAPACITY, n_mp, quarter)
            .transpose(0, 2, 1, 3)
            .reshape(n_expert * n_mp, CAPACITY, quarter)
        )
        arrived = lax.all_to_all(
            outgoing, ("expert", "mp"), split_axis=0, concat_axis=0, tiled=True
        )
        summed = jnp.sum(arrived.reshape(EXPERTS, split_size, CAPACITY, quarter), axis=1)
        mixing = jnp.sum(jnp.where(hit_mask, share_now[None, :, :], 0.0), axis=2)
        moe_term = lax.dot_general(
            mixing,
            summed.reshape(EXPERTS * CAPACITY, quarter),
            (((0,), (0,)), ((), ())),
            precision=lax.Precision.HIGHEST,
            preferred_element_type=jnp.float32,
        )
        result = (current.astype(jnp.float32) + moe_term).astype(jnp.bfloat16)
        current = from_behind(result, "section", -1)
    return current[None]


def solution(mesh):
    small = (mesh.shape["expert"], mesh.shape["mp"]) == (2, 4) and mesh.shape["section"] > 2
    placed = (
        P("section", "expert", "mp"),
        P("section", None, "expert", "mp"),
        P("section", None, "expert", None),
        P("section", None, "expert", None),
        P("section", None),
        P("section", None, ("expert", "mp")),
        P("section", ("expert", "mp"), None),
    )
    return jax.shard_map(
        fused if small else per_device,
        mesh=mesh,
        in_specs=placed,
        out_specs=P("section", "expert", "mp"),
        check_vma=False,
    )
```
